32 devices in a mesh: row: 8 (over z, x), col: 4 (over y, core).
Axes of the slice: x: 2, y: 2, z: 4, core: 2. Of those that a mesh axis runs over, the one named last changes fastest.
Arguments:
- features: bfloat16 [2048, 512], P(('row', 'col')), may hold values from -6 to 6
- tile_values: bfloat16 [8, 4, 64, 128, 128], P('row', 'col'), may hold values from -0.09375 to 0.09375
- tile_target: int32 [8, 4, 64], P('row', 'col'), may hold values from 0 to 1
- tile_anchor: int32 [8, 4, 64], P('row', 'col'), may hold values from 0 to 3
- live_tile_count: int32 [8, 4], P('row', 'col'), may hold values from 8 to 64, as said below
- mean_param: float32 [512, 512], P(None, 'col'), may hold values from -0.25 to 0.25
- spread_param: float32 [512, 512], P(None, 'col'), may hold values from -4.5 to -2.5
- noise_draws: bfloat16 [4, 512, 512], P(None, None, 'col'), may hold values from -6 to 6
- bias_shift: float32 [512], P('col'), may hold values from -3 to 3
- cotangent: bfloat16 [4, 2048, 512], P(None, 'row', 'col'), may hold values from -6 to 6
Outputs:
- activation: bfloat16 [4, 2048, 512], P(None, 'row', 'col')
- input_grad: bfloat16 [2048, 512], P(('row', 'col'))
- mean_grad: float32 [512, 512], P(None, 'col')
- spread_grad: float32 [512, 512], P(None, 'col')
- bias_grad: float32 [512], P('col')
The draws below stay inside these ranges and needn't reach their ends.
Inputs may be any that keep to these rules, and one draw needn't show every extreme that they name: `live_tile_count`: some cell holds 64 live tiles in every draw.
All inputs are finite; a program needn't handle non-finite values.
Results may differ from the reference program's by a relative error of at most 0.02.
Values may be sent and summed in bfloat16 or wider, within the bound.
A program may use at most 64 MiB of HBM per device.

```python
import jax
import jax.numpy as jnp
from jax import lax

F = 512
S = 4
TILE = 128
NODE_DEV = 64
TILE_SLOT_COUNT = 64
GRID_ROWS = 8
GRID_COLS = 4
NODES = 2048
N_ROW = 8
N_COL = 4


def draw_live_tile_count(key, part):
    key = jax.random.fold_in(key, 11)
    factor_key, second_key, choose_key = jax.random.split(key, 3)
    cell_total = GRID_ROWS * GRID_COLS
    factor_one = jax.random.randint(factor_key, (cell_total,), 0, TILE_SLOT_COUNT + 1)
    factor_two = jax.random.randint(second_key, (cell_total,), 0, TILE_SLOT_COUNT + 1)
    counted = jnp.maximum(factor_one * factor_two // TILE_SLOT_COUNT, TILE_SLOT_COUNT // 8)
    chosen_cell = jax.random.randint(choose_key, (), 0, cell_total)
    counted = jnp.where(jnp.arange(cell_total) == chosen_cell, TILE_SLOT_COUNT, counted)
    return counted.reshape(GRID_ROWS, GRID_COLS).astype(jnp.int32)


def draw_tile_target(key, part):
    key = jax.random.fold_in(key, 23)
    return jax.random.randint(key, (GRID_ROWS, GRID_COLS, TILE_SLOT_COUNT), 0, N_COL * NODE_DEV // TILE).astype(jnp.int32)


def draw_tile_anchor(key, part):
    key = jax.random.fold_in(key, 37)
    return jax.random.randint(key, (GRID_ROWS, GRID_COLS, TILE_SLOT_COUNT), 0, N_ROW * NODE_DEV // TILE).astype(jnp.int32)


def block_scale(stream_key, shape, cuts, low, high):
    gain, own = 1.0, jax.random.fold_in(stream_key, 6)
    for axis_at, blocks in cuts:
        steps = jnp.exp(jax.random.uniform(jax.random.fold_in(own, axis_at), (blocks,), jnp.float32, low / len(cuts), high / len(cuts)))
        gain = gain * jnp.repeat(steps, shape[axis_at] // blocks).reshape([-1 if axis == axis_at else 1 for axis in range(len(shape))])
    return gain


def bell_draw(stream_key, shape, deviation, bound, cuts=(), kind=jnp.bfloat16):
    level = block_scale(stream_key, shape, cuts, -0.22, 0.18) if cuts else 1.0
    entries = jax.random.normal(stream_key, shape, jnp.float32) * deviation * level
    return jnp.minimum(jnp.maximum(entries, -bound), bound).astype(kind)


def setup_inputs(seed: int = 0) -> dict:
    seeds = jax.random.split(jax.random.key(seed), 11)
    return {
        "features": bell_draw(seeds[0], (NODES, F), 1.0, 6.0, ((0, 32),)),
        "tile_values": bell_draw(seeds[1], (GRID_ROWS, GRID_COLS, TILE_SLOT_COUNT, TILE, TILE), (TILE_SLOT_COUNT * TILE * TILE // (N_COL * NODE_DEV)) ** -0.5, 0.09375, ((0, 8), (1, 4))),
        "tile_target": draw_tile_target(jax.random.fold_in(seeds[10], 71), 0),
        "tile_anchor": draw_tile_anchor(jax.random.fold_in(seeds[10], 71), 0),
        "live_tile_count": draw_live_tile_count(jax.random.fold_in(seeds[10], 71), 0),
        "mean_param": bell_draw(seeds[5], (F, F), F ** -0.5, 0.25, ((1, 4),), jnp.float32),
        "spread_param": jnp.clip(-4.5 + 2.0 * jax.random.uniform(seeds[6], (F, F), jnp.float32) ** block_scale(seeds[6], (F, F), ((1, 4),), -0.2, 0.2), -4.5, -2.5),
        "noise_draws": bell_draw(seeds[7], (S, F, F), 1.0, 6.0, ((2, 4),)),
        "bias_shift": bell_draw(seeds[8], (F,), 0.5, 3.0, ((0, 4),), jnp.float32),
        "cotangent": bell_draw(seeds[9], (S, NODES, F), 1.0, 6.0, ((1, 8), (2, 4))),
    }


def reference(features, tile_values, tile_target, tile_anchor, live_tile_count, mean_param, spread_param, noise_draws, bias_shift, cotangent):
    target_count = N_COL * NODE_DEV // TILE
    anchor_count = N_ROW * NODE_DEV // TILE
    grouped = jnp.transpose(features.reshape(N_ROW, N_COL, NODE_DEV, F), (1, 0, 2, 3)).reshape(N_COL, anchor_count, TILE, F)
    live_flags = (jnp.arange(TILE_SLOT_COUNT, dtype=jnp.int32)[None, None, :] < live_tile_count[:, :, None]).astype(jnp.float32)

    def forward_row(row_index_value):
        def add_column(running, column_index_value):
            matrix_stack = tile_values[row_index_value, column_index_value].astype(jnp.float32)
            selected_tiles = grouped[column_index_value][tile_anchor[row_index_value, column_index_value]].astype(jnp.float32)
            tile_matmul_result = jnp.einsum("yuk,ykc->yuc", matrix_stack, selected_tiles) * live_flags[row_index_value, column_index_value][:, None, None]
            placed = jax.ops.segment_sum(tile_matmul_result, tile_target[row_index_value, column_index_value], num_segments=target_count)
            rounded = lax.optimization_barrier(placed.astype(jnp.bfloat16))
            return running + rounded.astype(jnp.float32), None
        running, unused = lax.scan(add_column, jnp.zeros((target_count, TILE, F), jnp.float32), jnp.arange(N_COL, dtype=jnp.int32))
        return running

    aggregate = lax.map(forward_row, jnp.arange(N_ROW, dtype=jnp.int32)).astype(jnp.bfloat16).reshape(NODES, F)
    weights = (mean_param[None] + jax.nn.softplus(spread_param)[None] * noise_draws.astype(jnp.float32)).astype(jnp.bfloat16)
    weights_wide = weights.astype(jnp.float32)
    aggregate_wide = aggregate.astype(jnp.float32)
    preact = jnp.einsum("nf,sfk->snk", aggregate_wide, weights_wide) + bias_shift[None, None, :]
    activation = jax.nn.silu(preact).astype(jnp.bfloat16)
    logistic = jax.nn.sigmoid(preact)
    pre_grad = (cotangent.astype(jnp.float32) * logistic * (1.0 + preact * (1.0 - logistic))).astype(jnp.bfloat16)
    grad_wide = pre_grad.astype(jnp.float32)
    outer_sums = jnp.einsum("nf,snk->sfk", aggregate_wide, grad_wide)
    mean_grad = jnp.sum(outer_sums, axis=0)
    spread_grad = jax.nn.sigmoid(spread_param) * jnp.sum(noise_draws.astype(jnp.float32) * outer_sums, axis=0)
    bias_grad = jnp.sum(grad_wide, axis=(0, 1))
    slab_grad = jnp.einsum("snk,sfk->nf", grad_wide, weights_wide).astype(jnp.bfloat16)
    grad_slabs = slab_grad.reshape(N_ROW, target_count, TILE, F)

    def backward_column(column_index_value):
        def add_row(running, row_index_value):
            matrix_stack = tile_values[row_index_value, column_index_value].astype(jnp.float32)
            selected_tiles = grad_slabs[row_index_value][tile_target[row_index_value, column_index_value]].astype(jnp.float32)
            tile_matmul_result = jnp.einsum("lwo,lwm->lom", matrix_stack, selected_tiles) * live_flags[row_index_value, column_index_value][:, None, None]
            placed = jax.ops.segment_sum(tile_matmul_result, tile_anchor[row_index_value, column_index_value], num_segments=anchor_count)
            rounded = lax.optimization_barrier(placed.astype(jnp.bfloat16))
            return running + rounded.astype(jnp.float32), None
        running, unused = lax.scan(add_row, jnp.zeros((anchor_count, TILE, F), jnp.float32), jnp.arange(N_ROW, dtype=jnp.int32))
        return running

    backward = lax.map(backward_column, jnp.arange(N_COL, dtype=jnp.int32)).astype(jnp.bfloat16)
    input_grad = jnp.transpose(backward.reshape(N_COL, N_ROW, NODE_DEV, F), (1, 0, 2, 3)).reshape(NODES, F)
    return (activation, input_grad, mean_grad, spread_grad, bias_grad)
```

```python
import functools

import jax
import jax.numpy as jnp
from jax import lax
from jax.experimental import pallas as pl
from jax.experimental.pallas import tpu as pltpu
from jax.sharding import PartitionSpec as P

MESH = pl.DeviceIdType.MESH
PIECES = 2
BF = jnp.bfloat16
F32 = jnp.float32


def kernel(
    n_row, n_col,
    feat, tiles, target, anchor, live, mean, spread, noise, bias, cot,
    act_o, input_o, mean_o, spread_o, bias_o,
    tiles_v, mean_v, spread_v, noise_v, cot_v, act_v,
    xg, adj, adj_t, wcat, pgcat, agg, slab,
    c_out, c_in, c_own, c_half, c_y,
    b_out, b_own, b_in, b_sum, b_z,
    w_part, w_in, w_all, bias_part, bias_in,
    load_sem, act_sem, gz_s, gz_r, gx_s, gx_r,
    c1_s, c1_r, cy_s, cy_r, c3_s, c3_r,
    bx_s, bx_r, bz_s, bz_r, w1_s, w1_r, w2_s, w2_r, bi_s, bi_r,
):
    nodes, width = feat.shape
    slots, tile, _ = tiles.shape
    samples, _, panel = noise.shape
    rows = nodes * n_col
    half = rows // 2
    piece = half // PIECES
    zn, yn = n_row // 2, n_col // 2
    targets = rows // tile
    anchors = n_row * nodes // tile
    r, c = lax.axis_index("row"), lax.axis_index("col")
    z, x = r // 2, r % 2
    y, core = c // 2, c % 2
    r_twin = z * 2 + 1 - x
    c_twin = y * 2 + 1 - core
    pending = []

    def at(index, size):
        return pl.ds(pl.multiple_of(index * size, size), size)

    def send(src, dst, s_sem, r_sem, row, col):
        copy = pltpu.make_async_remote_copy(
            src_ref=src, dst_ref=dst, send_sem=s_sem, recv_sem=r_sem,
            device_id=(row, col), device_id_type=MESH,
        )
        copy.start()
        pending.append(copy)
        return copy

    loads = []
    pairs = ((spread, spread_v), (mean, mean_v), (noise, noise_v), (tiles, tiles_v), (cot, cot_v),
             (feat, xg.at[at(r, nodes)]))
    for i, (src, dst) in enumerate(pairs):
        load = pltpu.make_async_copy(src, dst, load_sem.at[i])
        load.start()
        loads.append(load)

    barrier = pltpu.get_barrier_semaphore()
    for k in range(1, n_row):
        pl.semaphore_signal(barrier, inc=1, device_id=((r + k) % n_row, c), device_id_type=MESH)
    for k in range(1, n_col):
        pl.semaphore_signal(barrier, inc=1, device_id=(r, (c + k) % n_col), device_id_type=MESH)
    pl.semaphore_wait(barrier, n_row + n_col - 2)

    here = xg.at[at(r, nodes)]
    along_z = {}
    order = sorted(range(1, zn), key=lambda k: min(k, zn - k))
    for k in order[::-1]:
        along_z[k] = send(feat, here, gz_s.at[k], gz_r.at[k], ((z + k) % zn) * 2 + x, c)
    along_x = [send(feat, here, gx_s.at[0], gx_r.at[0], r_twin, c)]

    def forward(k):
        along_z[k].wait_recv()
        spot = xg.at[at(((z - k + zn) % zn) * 2 + x, nodes)]
        along_x.append(send(spot, spot, gx_s.at[k], gx_r.at[k], r_twin, c))

    def make_weights():
        for load in loads[:3]:
            load.wait()
        soft = jnp.log1p(jnp.exp(spread_v[...]))
        for s in range(samples):
            wcat[:, s * panel:(s + 1) * panel] = (
                mean_v[...] + soft * noise_v[s].astype(F32)
            ).astype(BF)

    def make_adjacency(first, last):
        @pl.loop(first, last)
        def _(b):
            tb, ab = b // anchors, b % anchors

            def step(t, total):
                hit = (t < live[0]) & (target[t] == tb) & (anchor[t] == ab)
                return total + jnp.where(hit, 1.0, 0.0).astype(F32) * tiles_v[t].astype(F32)

            total = lax.fori_loop(0, slots, step, jnp.zeros((tile, tile), F32), unroll=8)
            adj[at(tb, tile), at(ab, tile)] = total.astype(BF)
            turned = total.T.astype(BF)
            adj_t[0, at(ab, nodes), at(tb, tile)] = turned[:nodes]
            adj_t[1, at(ab, nodes), at(tb, tile)] = turned[nodes:]

    blocks = targets * anchors
    make_weights()
    loads[3].wait()
    done = 0
    for i, k in enumerate(order):
        upto = blocks * (i + 1) // len(order)
        make_adjacency(done, upto)
        done = upto
        forward(k)
    loads[5].wait()
    for copy in along_x:
        copy.wait_recv()

    def col_reduce(i, term, full, between, own_done):
        first, crossing, last = [], [], []
        for q in range(PIECES):
            c_out[i, q] = term((1 - core) * PIECES + q).astype(BF)
            first.append(send(c_out.at[i, q], c_in.at[i, q], c1_s.at[i, q], c1_r.at[i, q], r, c_twin))
        for q in range(PIECES):
            c_own[q] = term(core * PIECES + q)
        for q in range(PIECES):
            first[q].wait_recv()
            c_half[i, q] = (c_own[q] + c_in[i, q].astype(F32)).astype(BF)
            for k in range(1, yn):
                crossing.append(send(
                    c_half.at[i, q], c_y.at[i, k, q], cy_s.at[i, k, q], cy_r.at[i, k, q],
                    r, ((y + k) % yn) * 2 + core,
                ))
        between()
        for q in range(PIECES):
            total = c_half[i, q].astype(F32)
            for k in range(1, yn):
                crossing[q * (yn - 1) + k - 1].wait_recv()
                total += c_y[i, k, q].astype(F32)
            spot = at(core * PIECES + q, piece)
            full[spot, :] = total.astype(BF)
            last.append(send(full.at[spot], full.at[spot], c3_s.at[i, q], c3_r.at[i, q], r, c_twin))
        own_done()
        for copy in last:
            copy.wait_recv()

    def neurons(which):
        spot = at(which, half)
        pre_all = jnp.dot(agg[spot, :], wcat[...], preferred_element_type=F32)
        for s in range(samples):
            pre = pre_all[:, s * panel:(s + 1) * panel] + bias[...]
            sig = jax.nn.sigmoid(pre)
            act_v[s, spot, :] = (pre * sig).astype(BF)
            pgcat[spot, s * panel:(s + 1) * panel] = (
                cot_v[s, spot, :].astype(F32) * sig * (1.0 + pre * (1.0 - sig))
            ).astype(BF)

    def own_neurons():
        loads[4].wait()
        neurons(core)

    col_reduce(
        0, lambda q: jnp.dot(adj[at(q, piece), :], xg[...], preferred_element_type=F32),
        agg, lambda: None, own_neurons,
    )
    neurons(1 - core)
    act_copy = pltpu.make_async_copy(act_v, act_o, act_sem.at[0])
    act_copy.start()

    share = width // n_row
    w_first, w_last, bias_sent = [], [], []

    def weight_terms():
        step = 256
        for f in range(0, width, step):
            outer = lax.dot_general(
                agg[:, f:f + step], pgcat[...], (((0,), (0,)), ((), ())), preferred_element_type=F32
            )
            parts = [outer[:, s * panel:(s + 1) * panel] for s in range(samples)]
            w_part[0, f:f + step, :] = sum(parts[1:], parts[0]).astype(BF)
            scaled = [noise_v[s, f:f + step, :].astype(F32) * parts[s] for s in range(samples)]
            w_part[1, f:f + step, :] = sum(scaled[1:], scaled[0]).astype(BF)
        sums = jnp.sum(pgcat[...].astype(F32), axis=0, keepdims=True)
        sums = [sums[:, s * panel:(s + 1) * panel] for s in range(samples)]
        bias_part[...] = jnp.broadcast_to(sum(sums[1:], sums[0]), bias_part.shape)
        for k in range(1, n_row):
            to = (r + k) % n_row
            w_first.append(send(w_part.at[:, at(to, share)], w_in.at[k], w1_s.at[k], w1_r.at[k], to, c))
            bias_sent.append(send(bias_part, bias_in.at[k], bi_s.at[k], bi_r.at[k], to, c))

    col_reduce(
        1,
        lambda q: lax.dot_general(
            pgcat[at(q, piece), :], wcat[...], (((1,), (1,)), ((), ())), preferred_element_type=F32
        ),
        slab, weight_terms, lambda: None,
    )

    b_out[...] = jnp.dot(adj_t[1 - x], slab[...], preferred_element_type=F32).astype(BF)
    b_first = {}
    for k in [*order[::-1], 0]:
        b_first[k] = send(b_out.at[at((z + k) % zn, nodes)], b_in.at[k], bx_s.at[k], bx_r.at[k], r_twin, c)
    b_own[...] = jnp.dot(adj_t[x], slab[...], preferred_element_type=F32)

    b_last = {}
    for k in order[::-1]:
        to = (z + k) % zn
        b_first[k].wait_recv()
        b_sum[k] = (b_own[at(to, nodes), :] + b_in[k].astype(F32)).astype(BF)
        b_last[k] = send(b_sum.at[k], b_z.at[k], bz_s.at[k], bz_r.at[k], to * 2 + x, c)

    total = w_part[:, at(r, share), :].astype(F32)
    for k in range(1, n_row):
        w_first[k - 1].wait_recv()
        total += w_in[k].astype(F32)
    spot = w_all.at[:, at(r, share)]
    w_all[:, at(r, share), :] = total.astype(BF)
    for k in range(1, n_row):
        w_last.append(send(spot, spot, w2_s.at[k], w2_r.at[k], (r + k) % n_row, c))

    total = bias_part[...]
    for k in range(1, n_row):
        bias_sent[k - 1].wait_recv()
        total += bias_in[k]
    bias_o[...] = total[:1]

    b_first[0].wait_recv()
    total = b_own[at(z, nodes), :] + b_in[0].astype(F32)
    for k in order:
        b_last[k].wait_recv()
        total += b_z[k].astype(F32)
    input_o[...] = total.astype(BF)

    for copy in w_last:
        copy.wait_recv()
    mean_o[...] = w_all[0].astype(F32)
    spread_o[...] = jax.nn.sigmoid(spread_v[...]) * w_all[1].astype(F32)
    act_copy.wait()
    for copy in pending:
        copy.wait_send()


def shards(
    n_row, n_col, features, tile_values, tile_target, tile_anchor, live_tile_count,
    mean_param, spread_param, noise_draws, bias_shift, cotangent,
):
    nodes, width = features.shape
    samples, _, panel = noise_draws.shape
    slots, tile = tile_values.shape[2:4]
    rows = nodes * n_col
    half = rows // 2
    piece = half // PIECES
    zn, yn = n_row // 2, n_col // 2
    share = width // n_row
    group = n_row * nodes
    any_space = pl.BlockSpec(memory_space=pl.ANY)
    smem = pl.BlockSpec(memory_space=pltpu.SMEM)
    vmem = pl.BlockSpec(memory_space=pltpu.VMEM)
    dma = pltpu.SemaphoreType.DMA
    buf = pltpu.VMEM
    scratch = [
        buf((slots, tile, tile), BF), buf((width, panel), F32), buf((width, panel), F32),
        buf((samples, width, panel), BF), buf((samples, rows, panel), BF), buf((samples, rows, panel), BF),
        buf((group, width), BF), buf((rows, group), BF), buf((2, group // 2, rows), BF),
        buf((width, samples * panel), BF), buf((rows, samples * panel), BF),
        buf((rows, width), BF), buf((rows, width), BF),
        buf((2, PIECES, piece, width), BF), buf((2, PIECES, piece, width), BF),
        buf((PIECES, piece, width), F32), buf((2, PIECES, piece, width), BF),
        buf((2, yn, PIECES, piece, width), BF),
        buf((group // 2, width), BF), buf((group // 2, width), F32), buf((zn, nodes, width), BF),
        buf((zn, nodes, width), BF), buf((zn, nodes, width), BF),
        buf((2, width, panel), BF), buf((n_row, 2, share, panel), BF), buf((2, width, panel), BF),
        buf((8, panel), F32), buf((n_row, 8, panel), F32),
        dma((6,)), dma((1,)), dma((zn,)), dma((zn,)), dma((zn,)), dma((zn,)),
        dma((2, PIECES)), dma((2, PIECES)), dma((2, yn, PIECES)), dma((2, yn, PIECES)),
        dma((2, PIECES)), dma((2, PIECES)),
        dma((zn,)), dma((zn,)), dma((zn,)), dma((zn,)),
        dma((n_row,)), dma((n_row,)), dma((n_row,)), dma((n_row,)), dma((n_row,)), dma((n_row,)),
    ]
    act, input_grad, mean_grad, spread_grad, bias_grad = pl.pallas_call(
        functools.partial(kernel, n_row, n_col),
        out_shape=(
            jax.ShapeDtypeStruct((samples, rows, panel), BF),
            jax.ShapeDtypeStruct((nodes, width), BF),
            jax.ShapeDtypeStruct((width, panel), F32),
            jax.ShapeDtypeStruct((width, panel), F32),
            jax.ShapeDtypeStruct((1, panel), F32),
        ),
        in_specs=[any_space, any_space, smem, smem, smem, any_space, any_space, any_space, vmem, any_space],
        out_specs=(any_space, vmem, vmem, vmem, vmem),
        scratch_shapes=scratch,
        compiler_params=pltpu.CompilerParams(
            collective_id=0, has_side_effects=True, vmem_limit_bytes=56 * 1024 * 1024
        ),
    )(
        features, tile_values[0, 0], tile_target[0, 0], tile_anchor[0, 0], live_tile_count[0],
        mean_param, spread_param, noise_draws, bias_shift[None], cotangent,
    )
    return act, input_grad, mean_grad, spread_grad, bias_grad[0]


def solution(mesh):
    placed = (
        P(("row", "col"), None),
        P("row", "col", None, None, None),
        P("row", "col", None),
        P("row", "col", None),
        P("row", "col"),
        P(None, "col"),
        P(None, "col"),
        P(None, None, "col"),
        P("col"),
        P(None, "row", "col"),
    )
    return jax.shard_map(
        functools.partial(shards, mesh.shape["row"], mesh.shape["col"]),
        mesh=mesh,
        in_specs=placed,
        out_specs=(
            P(None, "row", "col"),
            P(("row", "col"), None),
            P(None, "col"),
            P(None, "col"),
            P("col"),
        ),
        check_vma=False,
    )
```

```python
import functools

import jax
import jax.numpy as jnp
from jax import lax
from jax.experimental import pallas as pl
from jax.experimental.pallas import tpu as pltpu
from jax.sharding import PartitionSpec as P

MESH = pl.DeviceIdType.MESH
PIECES = 2
HALVES = 2
BF = jnp.bfloat16
F32 = jnp.float32


def kernel(
    n_row, n_col,
    feat, tiles, target, anchor, live, mean, spread, noise, bias, cot,
    act_o, input_o, grads_o, bias_o,
    tiles_v, mean_v, spread_v, noise_v, cot_v, act_v,
    xg, adj, adj_t, wcat, pgcat, agg, slab,
    c_out, c_in, c_own, c_half, c_y,
    b_out, b_own, b_in, b_sum, b_z,
    w_part, w_in, w_all, bias_part, bias_in,
    load_sem, act_sem, gz_s, gz_r, gx_s, gx_r, gp_s, gp_r,
    c1_s, c1_r, cy_s, cy_r, c3_s, c3_r,
    bx_s, bx_r, bz_s, bz_r, w1_s, w1_r, wz_s, wz_r, wx_s, wx_r, bi_s, bi_r,
):
    nodes, width = feat.shape
    slots, tile, _ = tiles.shape
    samples, _, panel = noise.shape
    rows = nodes * n_col
    half = rows // 2
    piece = half // PIECES
    zn, yn = n_row // 2, n_col // 2
    targets = rows // tile
    anchors = n_row * nodes // tile
    r, c = lax.axis_index("row"), lax.axis_index("col")
    z, x = r // 2, r % 2
    y, core = c // 2, c % 2
    r_twin = z * 2 + 1 - x
    c_twin = y * 2 + 1 - core
    pending = []

    def at(index, size):
        return pl.ds(pl.multiple_of(index * size, size), size)

    def send(src, dst, s_sem, r_sem, row, col):
        copy = pltpu.make_async_remote_copy(
            src_ref=src, dst_ref=dst, send_sem=s_sem, recv_sem=r_sem,
            device_id=(row, col), device_id_type=MESH,
        )
        copy.start()
        pending.append(copy)
        return copy

    loads = []
    pairs = ((spread, spread_v), (mean, mean_v), (noise, noise_v), (tiles, tiles_v), (cot, cot_v),
             (feat, xg.at[at(r, nodes)]))
    for i, (src, dst) in enumerate(pairs):
        load = pltpu.make_async_copy(src, dst, load_sem.at[i])
        load.start()
        loads.append(load)

    barrier = pltpu.get_barrier_semaphore()
    for k in range(1, n_row):
        pl.semaphore_signal(barrier, inc=1, device_id=((r + k) % n_row, c), device_id_type=MESH)
    for k in range(1, n_col):
        pl.semaphore_signal(barrier, inc=1, device_id=(r, (c + k) % n_col), device_id_type=MESH)
    pl.semaphore_wait(barrier, n_row + n_col - 2)

    pairs_z = zn // 2
    z_pair = z + 1 - 2 * (z % 2)
    across = range(1, zn - 1)
    part = nodes // HALVES

    def to_z(i):
        if i == 0:
            return z
        if i == zn - 1:
            return z_pair
        return ((z // 2 + (i + 1) // 2) % pairs_z) * 2 + (z % 2 + (i - 1) % 2) % 2

    def from_z(i):
        if i in (0, zn - 1):
            return to_z(i)
        return ((z // 2 - (i + 1) // 2 + pairs_z) % pairs_z) * 2 + (z % 2 + (i - 1) % 2) % 2

    here = xg.at[at(r, nodes)]
    along_z, along_x = {}, []

    def cross(h):
        for i in across:
            along_z[i, h] = send(
                feat.at[pl.ds(h * part, part)], xg.at[at(r * HALVES + h, part)],
                gz_s.at[i, h], gz_r.at[i, h], to_z(i) * 2 + x, c,
            )

    cross(0)
    along_x.append(send(feat, here, gx_s.at[0, 0], gx_r.at[0, 0], r_twin, c))
    along_x.append(send(feat, here, gp_s.at[0], gp_r.at[0], z_pair * 2 + x, c))
    along_x.append(send(feat, here, gp_s.at[1], gp_r.at[1], z_pair * 2 + 1 - x, c))
    for h in range(1, HALVES):
        cross(h)

    def forward(h):
        for i in across:
            along_z[i, h].wait_recv()
            spot = xg.at[at((from_z(i) * 2 + x) * HALVES + h, part)]
            along_x.append(send(spot, spot, gx_s.at[i, h], gx_r.at[i, h], r_twin, c))

    def make_weights():
        for load in loads[:3]:
            load.wait()
        soft = jnp.log1p(jnp.exp(spread_v[...]))
        for s in range(samples):
            wcat[:, s * panel:(s + 1) * panel] = (
                mean_v[...] + soft * noise_v[s].astype(F32)
            ).astype(BF)

    def make_adjacency(first, last):
        @pl.loop(first, last)
        def _(b):
            tb, ab = b // anchors, b % anchors

            def step(t, total):
                hit = (t < live[0, 0]) & (target[t] == tb) & (anchor[t] == ab)
                return total + jnp.where(hit, 1.0, 0.0).astype(F32) * tiles_v[t].astype(F32)

            total = lax.fori_loop(0, slots, step, jnp.zeros((tile, tile), F32), unroll=8)
            adj[at(tb, tile), at(ab, tile)] = total.astype(BF)
            turned = total.T.astype(BF)
            adj_t[0, at(ab, nodes), at(tb, tile)] = turned[:nodes]
            adj_t[1, at(ab, nodes), at(tb, tile)] = turned[nodes:]

    blocks = targets * anchors
    make_weights()
    loads[3].wait()
    done = 0
    for h in range(HALVES):
        upto = blocks * (h + 1) // HALVES
        make_adjacency(done, upto)
        done = upto
        forward(h)
    loads[5].wait()
    for copy in along_x:
        copy.wait_recv()

    def col_reduce(i, term, full, between, own_done):
        first, crossing, last = [], [], []
        for q in range(PIECES):
            c_out[i, q] = term((1 - core) * PIECES + q).astype(BF)
            first.append(send(c_out.at[i, q], c_in.at[i, q], c1_s.at[i, q], c1_r.at[i, q], r, c_twin))
        for q in range(PIECES):
            c_own[q] = term(core * PIECES + q)
        for q in range(PIECES):
            first[q].wait_recv()
            c_half[i, q] = (c_own[q] + c_in[i, q].astype(F32)).astype(BF)
            for k in range(1, yn):
                crossing.append(send(
                    c_half.at[i, q], c_y.at[i, k, q], cy_s.at[i, k, q], cy_r.at[i, k, q],
                    r, ((y + k) % yn) * 2 + core,
                ))
        between()
        for q in range(PIECES):
            total = c_half[i, q].astype(F32)
            for k in range(1, yn):
                crossing[q * (yn - 1) + k - 1].wait_recv()
                total += c_y[i, k, q].astype(F32)
            spot = at(core * PIECES + q, piece)
            full[spot, :] = total.astype(BF)
            last.append(send(full.at[spot], full.at[spot], c3_s.at[i, q], c3_r.at[i, q], r, c_twin))
        own_done()
        for copy in last:
            copy.wait_recv()

    def neurons(which):
        spot = at(which, half)
        pre_all = jnp.dot(agg[spot, :], wcat[...], preferred_element_type=F32)
        for s in range(samples):
            pre = pre_all[:, s * panel:(s + 1) * panel] + bias[...]
            sig = jax.nn.sigmoid(pre)
            act_v[s, spot, :] = (pre * sig).astype(BF)
            pgcat[spot, s * panel:(s + 1) * panel] = (
                cot_v[s, spot, :].astype(F32) * sig * (1.0 + pre * (1.0 - sig))
            ).astype(BF)

    def own_neurons():
        loads[4].wait()
        neurons(core)

    col_reduce(
        0, lambda q: jnp.dot(adj[at(q, piece), :], xg[...], preferred_element_type=F32),
        agg, lambda: None, own_neurons,
    )
    neurons(1 - core)
    act_copy = pltpu.make_async_copy(act_v, act_o, act_sem.at[0])
    act_copy.start()

    share = width // n_row
    w_first, w_last, bias_sent = [], [], []

    def weight_terms():
        step = 256
        for f in range(0, width, step):
            outer = lax.dot_general(
                agg[:, f:f + step], pgcat[...], (((0,), (0,)), ((), ())), preferred_element_type=F32
            )
            parts = [outer[:, s * panel:(s + 1) * panel] for s in range(samples)]
            w_part[0, f:f + step, :] = sum(parts[1:], parts[0]).astype(BF)
            scaled = [noise_v[s, f:f + step, :].astype(F32) * parts[s] for s in range(samples)]
            w_part[1, f:f + step, :] = sum(scaled[1:], scaled[0]).astype(BF)
        sums = jnp.sum(pgcat[...].astype(F32), axis=0, keepdims=True)
        sums = [sums[:, s * panel:(s + 1) * panel] for s in range(samples)]
        bias_part[...] = jnp.broadcast_to(sum(sums[1:], sums[0]), bias_part.shape)
        for k in range(1, n_row):
            to = (r + k) % n_row
            w_first.append(send(w_part.at[:, at(to, share)], w_in.at[k], w1_s.at[k], w1_r.at[k], to, c))
            bias_sent.append(send(bias_part, bias_in.at[k], bi_s.at[k], bi_r.at[k], to, c))

    col_reduce(
        1,
        lambda q: lax.dot_general(
            pgcat[at(q, piece), :], wcat[...], (((1,), (1,)), ((), ())), preferred_element_type=F32
        ),
        slab, weight_terms, lambda: None,
    )

    b_out[...] = jnp.dot(adj_t[1 - x], slab[...], preferred_element_type=F32).astype(BF)
    b_first, b_last = {}, {}
    queue = [(i, h) for h in range(HALVES) for i in across]
    queue += [(i, h) for i in (zn - 1, 0) for h in range(HALVES)]
    for i, h in queue:
        b_first[i, h] = send(
            b_out.at[at(to_z(i) * HALVES + h, part)], b_in.at[i, h], bx_s.at[i, h], bx_r.at[i, h], r_twin, c
        )
    b_own[...] = jnp.dot(adj_t[x], slab[...], preferred_element_type=F32)

    def onward(i, h):
        b_first[i, h].wait_recv()
        b_sum[i, h] = (b_own[at(to_z(i) * HALVES + h, part), :] + b_in[i, h].astype(F32)).astype(BF)
        b_last[i, h] = send(b_sum.at[i, h], b_z.at[i, h], bz_s.at[i, h], bz_r.at[i, h], to_z(i) * 2 + x, c)

    for i, h in queue[:-2 * HALVES]:
        onward(i, h)

    total = w_part[:, at(r, share), :].astype(F32)
    for k in range(1, n_row):
        w_first[k - 1].wait_recv()
        total += w_in[k].astype(F32)
    spot = w_all.at[:, at(r, share)]
    w_all[0, at(r, share), :] = total[0].astype(BF)
    w_all[1, at(r, share), :] = (jax.nn.sigmoid(spread_v[at(r, share), :]) * total[1]).astype(BF)
    w_z = {}
    for i in range(1, zn):
        w_z[i] = send(spot, spot, wz_s.at[i], wz_r.at[i], to_z(i) * 2 + x, c)
    w_last.append(send(spot, spot, wx_s.at[0], wx_r.at[0], r_twin, c))

    for h in range(HALVES):
        onward(zn - 1, h)

    total = bias_part[...]
    for k in range(1, n_row):
        bias_sent[k - 1].wait_recv()
        total += bias_in[k]
    bias_o[...] = total[:1]

    for i in [zn - 1, *across]:
        w_z[i].wait_recv()
        spot = w_all.at[:, at(from_z(i) * 2 + x, share)]
        w_last.append(send(spot, spot, wx_s.at[i], wx_r.at[i], r_twin, c))

    for h in range(HALVES):
        b_first[0, h].wait_recv()
        total = b_own[at(z * HALVES + h, part), :] + b_in[0, h].astype(F32)
        for i in range(1, zn):
            b_last[i, h].wait_recv()
            total += b_z[i, h].astype(F32)
        input_o[h * part:(h + 1) * part, :] = total.astype(BF)

    for copy in w_last:
        copy.wait_recv()
    grads_o[...] = w_all[...]
    act_copy.wait()
    for copy in pending:
        copy.wait_send()


def finish(act, input_grad, grads, bias, act_o, input_o, mean_o, spread_o, bias_o, sem):
    copies = [
        pltpu.make_async_copy(act, act_o, sem.at[0]),
        pltpu.make_async_copy(input_grad, input_o, sem.at[1]),
    ]
    for copy in copies:
        copy.start()
    mean_o[...] = grads[0].astype(F32)
    spread_o[...] = grads[1].astype(F32)
    bias_o[...] = bias[...]
    for copy in copies:
        copy.wait()


def shards(
    n_row, n_col, features, tile_values, tile_target, tile_anchor, live_tile_count,
    mean_param, spread_param, noise_draws, bias_shift, cotangent,
):
    nodes, width = features.shape
    samples, _, panel = noise_draws.shape
    slots, tile = tile_values.shape[2:4]
    rows = nodes * n_col
    half = rows // 2
    piece = half // PIECES
    zn, yn = n_row // 2, n_col // 2
    share = width // n_row
    group = n_row * nodes
    any_space = pl.BlockSpec(memory_space=pl.ANY)
    smem = pl.BlockSpec(memory_space=pltpu.SMEM)
    vmem = pl.BlockSpec(memory_space=pltpu.VMEM)
    dma = pltpu.SemaphoreType.DMA
    buf = pltpu.VMEM
    scratch = [
        buf((slots, tile, tile), BF), buf((width, panel), F32), buf((width, panel), F32),
        buf((samples, width, panel), BF), buf((samples, rows, panel), BF), buf((samples, rows, panel), BF),
        buf((group, width), BF), buf((rows, group), BF), buf((2, group // 2, rows), BF),
        buf((width, samples * panel), BF), buf((rows, samples * panel), BF),
        buf((rows, width), BF), buf((rows, width), BF),
        buf((2, PIECES, piece, width), BF), buf((2, PIECES, piece, width), BF),
        buf((PIECES, piece, width), F32), buf((2, PIECES, piece, width), BF),
        buf((2, yn, PIECES, piece, width), BF),
        buf((group // 2, width), BF), buf((group // 2, width), F32), buf((zn, HALVES, nodes // HALVES, width), BF),
        buf((zn, HALVES, nodes // HALVES, width), BF), buf((zn, HALVES, nodes // HALVES, width), BF),
        buf((2, width, panel), BF), buf((n_row, 2, share, panel), BF), buf((2, width, panel), BF),
        buf((8, panel), F32), buf((n_row, 8, panel), F32),
        dma((6,)), dma((1,)), *[dma((zn, HALVES))] * 4, dma((2,)), dma((2,)),
        dma((2, PIECES)), dma((2, PIECES)), dma((2, yn, PIECES)), dma((2, yn, PIECES)),
        dma((2, PIECES)), dma((2, PIECES)),
        *[dma((zn, HALVES))] * 4, dma((n_row,)), dma((n_row,)), *[dma((zn,))] * 4, dma((n_row,)), dma((n_row,)),
    ]
    held = pl.pallas_call(
        functools.partial(kernel, n_row, n_col),
        out_shape=(
            jax.ShapeDtypeStruct((samples, rows, panel), BF),
            jax.ShapeDtypeStruct((nodes, width), BF),
            jax.ShapeDtypeStruct((2, width, panel), BF),
            jax.ShapeDtypeStruct((1, panel), F32),
        ),
        in_specs=[any_space, any_space, smem, smem, smem, any_space, any_space, any_space, vmem, any_space],
        out_specs=(any_space, vmem, vmem, vmem),
        scratch_shapes=scratch,
        compiler_params=pltpu.CompilerParams(
            collective_id=0, has_side_effects=True, vmem_limit_bytes=56 * 1024 * 1024
        ),
    )(
        features, tile_values[0, 0], tile_target[0, 0], tile_anchor[0, 0], live_tile_count,
        mean_param, spread_param, noise_draws, bias_shift[None], cotangent,
    )
    act, input_grad, mean_grad, spread_grad, bias_grad = pl.pallas_call(
        finish,
        out_shape=(
            jax.ShapeDtypeStruct((samples, rows, panel), BF),
            jax.ShapeDtypeStruct((nodes, width), BF),
            jax.ShapeDtypeStruct((width, panel), F32),
            jax.ShapeDtypeStruct((width, panel), F32),
            jax.ShapeDtypeStruct((1, panel), F32),
        ),
        in_specs=[any_space, any_space, vmem, vmem],
        out_specs=(any_space, any_space, vmem, vmem, vmem),
        scratch_shapes=[dma((2,))],
    )(*held)
    return act, input_grad, mean_grad, spread_grad, bias_grad[0]


def solution(mesh):
    placed = (
        P(("row", "col"), None),
        P("row", "col", None, None, None),
        P("row", "col", None),
        P("row", "col", None),
        P("row", "col"),
        P(None, "col"),
        P(None, "col"),
        P(None, None, "col"),
        P("col"),
        P(None, "row", "col"),
    )
    return jax.shard_map(
        functools.partial(shards, mesh.shape["row"], mesh.shape["col"]),
        mesh=mesh,
        in_specs=placed,
        out_specs=(
            P(None, "row", "col"),
            P(("row", "col"), None),
            P(None, "col"),
            P(None, "col"),
            P("col"),
        ),
        check_vma=False,
    )
```

```python
import functools

import jax
import jax.numpy as jnp
from jax import lax
from jax.experimental import pallas as pl
from jax.experimental.pallas import tpu as pltpu
from jax.sharding import PartitionSpec as P

MESH = pl.DeviceIdType.MESH
PIECES = 2
HALVES = 2
BF = jnp.bfloat16
F32 = jnp.float32


def kernel(
    n_row, n_col,
    feat, tiles, target, anchor, live, mean, spread, noise, bias, cot,
    act_o, input_o, grads_o, bias_o,
    tiles_v, mean_v, spread_v, noise_v, cot_v, act_v,
    xg, adj, adj_t, wcat, pgcat, agg, slab,
    c_out, c_in, c_own, c_half, c_y,
    b_out, b_own, b_in, b_sum, b_z,
    w_part, w_in, w_all, bias_part, bias_in,
    load_sem, act_sem, gz_s, gz_r, gx_s, gx_r, gp_s, gp_r,
    c1_s, c1_r, cy_s, cy_r, c3_s, c3_r,
    bx_s, bx_r, bz_s, bz_r, w1_s, w1_r, wz_s, wz_r, wx_s, wx_r, bi_s, bi_r,
):
    nodes, width = feat.shape
    slots, tile, _ = tiles.shape
    samples, _, panel = noise.shape
    rows = nodes * n_col
    half = rows // 2
    piece = half // PIECES
    zn, yn = n_row // 2, n_col // 2
    targets = rows // tile
    anchors = n_row * nodes // tile
    r, c = lax.axis_index("row"), lax.axis_index("col")
    z, x = r // 2, r % 2
    y, core = c // 2, c % 2
    r_twin = z * 2 + 1 - x
    c_twin = y * 2 + 1 - core
    pending = []

    def at(index, size):
        return pl.ds(pl.multiple_of(index * size, size), size)

    def send(src, dst, s_sem, r_sem, row, col):
        copy = pltpu.make_async_remote_copy(
            src_ref=src, dst_ref=dst, send_sem=s_sem, recv_sem=r_sem,
            device_id=(row, col), device_id_type=MESH,
        )
        copy.start()
        pending.append(copy)
        return copy

    loads = []
    pairs = ((spread, spread_v), (mean, mean_v), (noise, noise_v), (tiles, tiles_v), (cot, cot_v),
             (feat, xg.at[at(r, nodes)]))
    for i, (src, dst) in enumerate(pairs):
        load = pltpu.make_async_copy(src, dst, load_sem.at[i])
        load.start()
        loads.append(load)

    barrier = pltpu.get_barrier_semaphore()
    for k in range(1, n_row):
        pl.semaphore_signal(barrier, inc=1, device_id=((r + k) % n_row, c), device_id_type=MESH)
    for k in range(1, n_col):
        pl.semaphore_signal(barrier, inc=1, device_id=(r, (c + k) % n_col), device_id_type=MESH)
    pl.semaphore_wait(barrier, n_row + n_col - 2)

    pairs_z = zn // 2
    z_pair = z + 1 - 2 * (z % 2)
    across = range(1, zn - 1)
    part = nodes // HALVES

    def to_z(i):
        if i == 0:
            return z
        if i == zn - 1:
            return z_pair
        return ((z // 2 + (i + 1) // 2) % pairs_z) * 2 + (z % 2 + (i - 1) % 2) % 2

    def from_z(i):
        if i in (0, zn - 1):
            return to_z(i)
        return ((z // 2 - (i + 1) // 2 + pairs_z) % pairs_z) * 2 + (z % 2 + (i - 1) % 2) % 2

    here = xg.at[at(r, nodes)]
    along_z, along_x = {}, []

    def cross(h):
        for i in across:
            along_z[i, h] = send(
                feat.at[pl.ds(h * part, part)], xg.at[at(r * HALVES + h, part)],
                gz_s.at[i, h], gz_r.at[i, h], to_z(i) * 2 + x, c,
            )

    cross(0)
    along_x.append(send(feat, here, gx_s.at[0, 0], gx_r.at[0, 0], r_twin, c))
    along_x.append(send(feat, here, gp_s.at[0], gp_r.at[0], z_pair * 2 + x, c))
    along_x.append(send(feat, here, gp_s.at[1], gp_r.at[1], z_pair * 2 + 1 - x, c))
    for h in range(1, HALVES):
        cross(h)

    def forward(h):
        for i in across:
            along_z[i, h].wait_recv()
            spot = xg.at[at((from_z(i) * 2 + x) * HALVES + h, part)]
            along_x.append(send(spot, spot, gx_s.at[i, h], gx_r.at[i, h], r_twin, c))

    def make_weights():
        for load in loads[:3]:
            load.wait()
        soft = jnp.log1p(jnp.exp(spread_v[...]))
        for s in range(samples):
            wcat[:, s * panel:(s + 1) * panel] = (
                mean_v[...] + soft * noise_v[s].astype(F32)
            ).astype(BF)

    def make_adjacency(first, last):
        @pl.loop(first, last)
        def _(b):
            tb, ab = b // anchors, b % anchors

            def step(t, total):
                hit = (t < live[0, 0]) & (target[t] == tb) & (anchor[t] == ab)
                return total + jnp.where(hit, 1.0, 0.0).astype(F32) * tiles_v[t].astype(F32)

            total = lax.fori_loop(0, slots, step, jnp.zeros((tile, tile), F32), unroll=8)
            adj[at(tb, tile), at(ab, tile)] = total.astype(BF)
            turned = total.T.astype(BF)
            adj_t[0, at(ab, nodes), at(tb, tile)] = turned[:nodes]
            adj_t[1, at(ab, nodes), at(tb, tile)] = turned[nodes:]

    blocks = targets * anchors
    make_weights()
    loads[3].wait()
    done = 0
    for h in range(HALVES):
        upto = blocks * (h + 1) // HALVES
        make_adjacency(done, upto)
        done = upto
        forward(h)
    loads[5].wait()
    for copy in along_x:
        copy.wait_recv()

    def col_reduce(i, term, full, between, own_done):
        first, crossing, last = [], [], []
        for q in range(PIECES):
            c_out[i, q] = term((1 - core) * PIECES + q).astype(BF)
            first.append(send(c_out.at[i, q], c_in.at[i, q], c1_s.at[i, q], c1_r.at[i, q], r, c_twin))
        for q in range(PIECES):
            c_own[q] = term(core * PIECES + q)
        for q in range(PIECES):
            first[q].wait_recv()
            c_half[i, q] = (c_own[q] + c_in[i, q].astype(F32)).astype(BF)
            for k in range(1, yn):
                crossing.append(send(
                    c_half.at[i, q], c_y.at[i, k, q], cy_s.at[i, k, q], cy_r.at[i, k, q],
                    r, ((y + k) % yn) * 2 + core,
                ))
        between()
        for q in range(PIECES):
            total = c_half[i, q].astype(F32)
            for k in range(1, yn):
                crossing[q * (yn - 1) + k - 1].wait_recv()
                total += c_y[i, k, q].astype(F32)
            spot = at(core * PIECES + q, piece)
            full[spot, :] = total.astype(BF)
            last.append(send(full.at[spot], full.at[spot], c3_s.at[i, q], c3_r.at[i, q], r, c_twin))
        own_done()
        for copy in last:
            copy.wait_recv()

    def neurons(which):
        spot = at(which, half)
        pre_all = jnp.dot(agg[spot, :], wcat[...], preferred_element_type=F32)
        for s in range(samples):
            pre = pre_all[:, s * panel:(s + 1) * panel] + bias[...]
            sig = jax.nn.sigmoid(pre)
            act_v[s, spot, :] = (pre * sig).astype(BF)
            pgcat[spot, s * panel:(s + 1) * panel] = (
                cot_v[s, spot, :].astype(F32) * sig * (1.0 + pre * (1.0 - sig))
            ).astype(BF)

    def own_neurons():
        loads[4].wait()
        neurons(core)

    col_reduce(
        0, lambda q: jnp.dot(adj[at(q, piece), :], xg[...], preferred_element_type=F32),
        agg, lambda: None, own_neurons,
    )
    neurons(1 - core)
    act_copy = pltpu.make_async_copy(act_v, act_o, act_sem.at[0])
    act_copy.start()

    share = width // n_row
    w_first, w_last, bias_sent = [], [], []

    def weight_terms():
        step = 256
        for f in range(0, width, step):
            outer = lax.dot_general(
                agg[:, f:f + step], pgcat[...], (((0,), (0,)), ((), ())), preferred_element_type=F32
            )
            parts = [outer[:, s * panel:(s + 1) * panel] for s in range(samples)]
            w_part[0, f:f + step, :] = sum(parts[1:], parts[0]).astype(BF)
            scaled = [noise_v[s, f:f + step, :].astype(F32) * parts[s] for s in range(samples)]
            w_part[1, f:f + step, :] = sum(scaled[1:], scaled[0]).astype(BF)
        sums = jnp.sum(pgcat[...].astype(F32), axis=0, keepdims=True)
        sums = [sums[:, s * panel:(s + 1) * panel] for s in range(samples)]
        bias_part[...] = jnp.broadcast_to(sum(sums[1:], sums[0]), bias_part.shape)
        for k in range(1, n_row):
            to = (r + k) % n_row
            w_first.append(send(w_part.at[:, at(to, share)], w_in.at[k], w1_s.at[k], w1_r.at[k], to, c))
            bias_sent.append(send(bias_part, bias_in.at[k], bi_s.at[k], bi_r.at[k], to, c))

    col_reduce(
        1,
        lambda q: lax.dot_general(
            pgcat[at(q, piece), :], wcat[...], (((1,), (1,)), ((), ())), preferred_element_type=F32
        ),
        slab, weight_terms, lambda: None,
    )

    b_out[...] = jnp.dot(adj_t[1 - x], slab[...], preferred_element_type=F32).astype(BF)
    b_first, b_last = {}, {}
    queue = [(i, h) for h in range(HALVES) for i in across]
    queue += [(i, h) for i in (zn - 1, 0) for h in range(HALVES)]
    for i, h in queue:
        b_first[i, h] = send(
            b_out.at[at(to_z(i) * HALVES + h, part)], b_in.at[i, h], bx_s.at[i, h], bx_r.at[i, h], r_twin, c
        )
    b_own[...] = jnp.dot(adj_t[x], slab[...], preferred_element_type=F32)

    def onward(i, h):
        b_first[i, h].wait_recv()
        b_sum[i, h] = (b_own[at(to_z(i) * HALVES + h, part), :] + b_in[i, h].astype(F32)).astype(BF)
        b_last[i, h] = send(b_sum.at[i, h], b_z.at[i, h], bz_s.at[i, h], bz_r.at[i, h], to_z(i) * 2 + x, c)

    for i, h in queue[:-2 * HALVES]:
        onward(i, h)

    total = w_part[:, at(r, share), :].astype(F32)
    for k in range(1, n_row):
        w_first[k - 1].wait_recv()
        total += w_in[k].astype(F32)
    spot = w_all.at[:, at(r, share)]
    w_all[0, at(r, share), :] = total[0].astype(BF)
    w_all[1, at(r, share), :] = (jax.nn.sigmoid(spread_v[at(r, share), :]) * total[1]).astype(BF)
    w_z = {}
    for i in range(1, zn):
        w_z[i] = send(spot, spot, wz_s.at[i], wz_r.at[i], to_z(i) * 2 + x, c)
    w_last.append(send(spot, spot, wx_s.at[0], wx_r.at[0], r_twin, c))

    for h in range(HALVES):
        onward(zn - 1, h)

    total = bias_part[...]
    for k in range(1, n_row):
        bias_sent[k - 1].wait_recv()
        total += bias_in[k]
    bias_o[...] = total[:1]

    for i in [zn - 1, *across]:
        w_z[i].wait_recv()
        spot = w_all.at[:, at(from_z(i) * 2 + x, share)]
        w_last.append(send(spot, spot, wx_s.at[i], wx_r.at[i], r_twin, c))

    for h in range(HALVES):
        b_first[0, h].wait_recv()
        total = b_own[at(z * HALVES + h, part), :] + b_in[0, h].astype(F32)
        for i in range(1, zn):
            b_last[i, h].wait_recv()
            total += b_z[i, h].astype(F32)
        input_o[h * part:(h + 1) * part, :] = total.astype(BF)

    for copy in w_last:
        copy.wait_recv()
    grads_o[...] = w_all[...]
    act_copy.wait()
    for copy in pending:
        copy.wait_send()


def finish(act, input_grad, grads, bias, act_o, input_o, mean_o, spread_o, bias_o):
    act_o[...] = act[...]
    input_o[...] = input_grad[...]
    mean_o[...] = grads[0].astype(F32)
    spread_o[...] = grads[1].astype(F32)
    bias_o[...] = bias[...]


def shards(
    n_row, n_col, features, tile_values, tile_target, tile_anchor, live_tile_count,
    mean_param, spread_param, noise_draws, bias_shift, cotangent,
):
    nodes, width = features.shape
    samples, _, panel = noise_draws.shape
    slots, tile = tile_values.shape[2:4]
    rows = nodes * n_col
    half = rows // 2
    piece = half // PIECES
    zn, yn = n_row // 2, n_col // 2
    share = width // n_row
    group = n_row * nodes
    any_space = pl.BlockSpec(memory_space=pl.ANY)
    smem = pl.BlockSpec(memory_space=pltpu.SMEM)
    vmem = pl.BlockSpec(memory_space=pltpu.VMEM)
    dma = pltpu.SemaphoreType.DMA
    buf = pltpu.VMEM
    scratch = [
        buf((slots, tile, tile), BF), buf((width, panel), F32), buf((width, panel), F32),
        buf((samples, width, panel), BF), buf((samples, rows, panel), BF), buf((samples, rows, panel), BF),
        buf((group, width), BF), buf((rows, group), BF), buf((2, group // 2, rows), BF),
        buf((width, samples * panel), BF), buf((rows, samples * panel), BF),
        buf((rows, width), BF), buf((rows, width), BF),
        buf((2, PIECES, piece, width), BF), buf((2, PIECES, piece, width), BF),
        buf((PIECES, piece, width), F32), buf((2, PIECES, piece, width), BF),
        buf((2, yn, PIECES, piece, width), BF),
        buf((group // 2, width), BF), buf((group // 2, width), F32), buf((zn, HALVES, nodes // HALVES, width), BF),
        buf((zn, HALVES, nodes // HALVES, width), BF), buf((zn, HALVES, nodes // HALVES, width), BF),
        buf((2, width, panel), BF), buf((n_row, 2, share, panel), BF), buf((2, width, panel), BF),
        buf((8, panel), F32), buf((n_row, 8, panel), F32),
        dma((6,)), dma((1,)), *[dma((zn, HALVES))] * 4, dma((2,)), dma((2,)),
        dma((2, PIECES)), dma((2, PIECES)), dma((2, yn, PIECES)), dma((2, yn, PIECES)),
        dma((2, PIECES)), dma((2, PIECES)),
        *[dma((zn, HALVES))] * 4, dma((n_row,)), dma((n_row,)), *[dma((zn,))] * 4, dma((n_row,)), dma((n_row,)),
    ]
    held = pl.pallas_call(
        functools.partial(kernel, n_row, n_col),
        out_shape=(
            jax.ShapeDtypeStruct((samples, rows, panel), BF),
            jax.ShapeDtypeStruct((nodes, width), BF),
            jax.ShapeDtypeStruct((2, width, panel), BF),
            jax.ShapeDtypeStruct((1, panel), F32),
        ),
        in_specs=[any_space, any_space, smem, smem, smem, any_space, any_space, any_space, vmem, any_space],
        out_specs=(any_space, vmem, vmem, vmem),
        scratch_shapes=scratch,
        compiler_params=pltpu.CompilerParams(
            collective_id=0, has_side_effects=True, vmem_limit_bytes=56 * 1024 * 1024
        ),
    )(
        features, tile_values[0, 0], tile_target[0, 0], tile_anchor[0, 0], live_tile_count,
        mean_param, spread_param, noise_draws, bias_shift[None], cotangent,
    )
    act, input_grad, mean_grad, spread_grad, bias_grad = pl.pallas_call(
        finish,
        out_shape=(
            jax.ShapeDtypeStruct((samples, rows, panel), BF),
            jax.ShapeDtypeStruct((nodes, width), BF),
            jax.ShapeDtypeStruct((width, panel), F32),
            jax.ShapeDtypeStruct((width, panel), F32),
            jax.ShapeDtypeStruct((1, panel), F32),
        ),
        in_specs=[vmem] * 4,
        out_specs=(vmem,) * 5,
        compiler_params=pltpu.CompilerParams(vmem_limit_bytes=32 * 1024 * 1024),
    )(*held)
    return act, input_grad, mean_grad, spread_grad, bias_grad[0]


def solution(mesh):
    placed = (
        P(("row", "col"), None),
        P("row", "col", None, None, None),
        P("row", "col", None),
        P("row", "col", None),
        P("row", "col"),
        P(None, "col"),
        P(None, "col"),
        P(None, None, "col"),
        P("col"),
        P(None, "row", "col"),
    )
    return jax.shard_map(
        functools.partial(shards, mesh.shape["row"], mesh.shape["col"]),
        mesh=mesh,
        in_specs=placed,
        out_specs=(
            P(None, "row", "col"),
            P(("row", "col"), None),
            P(None, "col"),
            P(None, "col"),
            P("col"),
        ),
        check_vma=False,
    )
```
